256 devices in a mesh: space: 128 (over z, y, x_hi, core), blk: 2 (over x_lo).
Axes of the slice: x: 4 (x_hi: 2, x_lo: 2; x = x_hi * 2 + x_lo), y: 4, z: 8, core: 2. Of those that a mesh axis runs over, the one named last changes fastest.
Arguments:
- record: bfloat16 [32, 128, 196608], P('blk', None, 'space'), may hold values from -10 to 10, as said below
- weights: float32 [196608], P('space'), may hold values from 0.0625 to 9
Outputs:
- modes: bfloat16 [64, 2, 32, 196608], P('blk', None, None, 'space')
- energies: float32 [64, 64], P('blk')
The draws below stay inside these ranges and needn't reach their ends.
Inputs may be any that keep to these rules, and one draw needn't show every extreme that they name: `record`: the snapshots of all blocks share a common part.
All inputs are finite; a program needn't handle non-finite values.
Results may differ from the reference program's by a relative error of at most 0.0073.
Values may be sent and summed in bfloat16 or wider, within the bound.
No kernel may reach another device: no remote copies, remote signals or barrier semaphores. Data moves between devices by JAX's collectives and lax.ppermute only.
A program may use at most 128 MiB of HBM per device.

```python
import math
import jax
import jax.numpy as jnp
from jax import lax

NB = 32
NT = 128
NF = 64
NP = 196608


def draw_record(key, part):
    key = jax.random.fold_in(key, 11)
    key_noise, key_common, key_gains, key_delay = jax.random.split(key, 4)
    delays = jax.random.randint(key_delay, (NB,), 0, NT).astype(jnp.int32)
    time_rows = (jnp.arange(NT, dtype=jnp.int32)[None, :] - delays[:, None]) % NT
    noise = jnp.clip(jax.random.normal(key_noise, (NB, NT, NP), jnp.float32), -4.0, 4.0)
    common = jnp.clip(jax.random.normal(key_common, (NT, NP), jnp.float32), -4.0, 4.0)
    gains = jax.random.uniform(key_gains, (NB, 1, 1), jnp.float32, 0.5, 1.5)
    delayed = jnp.take(common, time_rows, axis=0)
    return (noise + gains * delayed).astype(jnp.bfloat16)


def draw_weights(key, part):
    key = jax.random.fold_in(key, 23)
    position = jnp.arange(NP, dtype=jnp.float32) / NP
    rough = jnp.exp(jax.random.uniform(key, (NP,), jnp.float32, 0.0, math.log(10.0)))
    return ((1.0 + 2.0 * position) * rough / 8.0).astype(jnp.float32)


def setup_inputs(seed: int = 0) -> dict:
    keys = jax.random.split(jax.random.key(seed), 3)
    return {
        "record": draw_record(jax.random.fold_in(keys[2], 71), 0),
        "weights": draw_weights(jax.random.fold_in(keys[2], 71), 0),
    }


def spectral_table(freq_count, time_steps):
    time_index = jnp.arange(time_steps, dtype=jnp.int32)
    freq_index = jnp.arange(freq_count, dtype=jnp.int32)
    phases = (freq_index[:, None] * time_index[None, :] % time_steps).astype(jnp.float32) * (2.0 * math.pi / time_steps)
    window = 0.5 - 0.5 * jnp.cos(time_index.astype(jnp.float32) * (2.0 * math.pi / time_steps))
    window_norm = jnp.sqrt(jnp.sum(window * window))
    rows_cos = window * jnp.cos(phases) / window_norm
    rows_sin = -window * jnp.sin(phases) / window_norm
    return jnp.stack([rows_cos, rows_sin], axis=1).astype(jnp.bfloat16)

def whiten(real_part, imag_part, spectra):
    embedded = jnp.concatenate([jnp.concatenate([real_part, -imag_part], axis=-1), jnp.concatenate([imag_part, real_part], axis=-1)], axis=-2)
    factor = jnp.linalg.cholesky(embedded)
    energies = jnp.diagonal(factor, axis1=-2, axis2=-1) ** 2
    values = spectra.astype(jnp.float32)
    first = jnp.concatenate([values[0], -values[1]], axis=0)
    second = jnp.concatenate([values[1], values[0]], axis=0)
    stacked = jnp.stack([first, second], axis=0)
    blocks = real_part.shape[0]
    factors = jnp.broadcast_to(factor, (2,) + factor.shape)
    solved = lax.linalg.triangular_solve(factors, stacked, left_side=True, lower=True)
    return (energies, solved[:, blocks:, :].astype(jnp.bfloat16))

def reference(record, weights):
    table = spectral_table(NF, NT)

    def one_freq(rows):
        spectra = jnp.dot(rows.astype(jnp.float32), record.astype(jnp.float32), preferred_element_type=jnp.float32).astype(jnp.bfloat16)
        weighted = (spectra.astype(jnp.float32) * weights).astype(jnp.bfloat16)
        gram = jnp.einsum('cip,djp->cidj', spectra.astype(jnp.float32), weighted.astype(jnp.float32), precision=lax.Precision.HIGHEST)
        real_part = (gram[0, :, 0, :] + gram[1, :, 1, :]) / NP
        imag_part = (gram[0, :, 1, :] - gram[1, :, 0, :]) / NP
        return whiten(real_part, imag_part, spectra)
    energies, modes = lax.map(one_freq, table)
    return (modes, energies)
```

```python
import functools
import math

import jax
import jax.numpy as jnp
import numpy as np
from jax import lax
from jax.experimental import pallas as pl
from jax.experimental.pallas import tpu as pltpu
from jax.sharding import Mesh
from jax.sharding import PartitionSpec as P

NF = 64
NT = 128
GROUPS = (1, 1, 2)
FINE = ("z", "y", "xh", "core", "blk")
AHEAD = 3
MIB = 1024 * 1024


def spectral_table():
    time_index = np.arange(NT, dtype=np.int32)
    freq_index = np.arange(NF, dtype=np.int32)
    step = np.float32(2.0 * math.pi / NT)
    phases = (freq_index[:, None] * time_index[None, :] % NT).astype(np.float32) * step
    window = np.float32(0.5) - np.float32(0.5) * np.cos(time_index.astype(np.float32) * step)
    norm = np.sqrt(np.sum(window * window))
    rows_cos = window * np.cos(phases) / norm
    rows_sin = -window * np.sin(phases) / norm
    return np.stack([rows_cos, rows_sin], axis=1).astype(jnp.bfloat16)


def pair_table(first_owner):
    table = spectral_table().reshape(2, 4, 8, 2, NT)
    out = np.zeros((2, 4, 2, 2, 8, 2, NT), dtype=table.dtype)
    for b in range(2):
        out[:, :, :, b, :, b, :] = table.transpose(0, 1, 3, 2, 4)
    if first_owner:
        out = out[::-1]
    return np.ascontiguousarray(out).reshape(256, 256)


def early_kernel(first, owner_ref, tables_ref, record_ref, out_ref, table, rows, table_sem, sems):
    pairs, _, _, points = rows.shape
    head = pltpu.make_async_copy(tables_ref.at[owner_ref[0]], table, table_sem)
    head.start()
    copies = [
        pltpu.make_async_copy(
            record_ref.at[pl.ds(2 * (first + p), 2)], rows.at[p], sems.at[p]
        )
        for p in range(pairs)
    ]
    for p in range(min(4, pairs)):
        copies[p].start()
    head.wait()
    left = table[...]
    for p in range(pairs):
        copies[p].wait()
        if p + 4 < pairs:
            copies[p + 4].start()
        value = jnp.dot(
            left, rows[p].reshape(256, points), preferred_element_type=jnp.float32
        ).astype(jnp.bfloat16)
        for row in range(0, value.shape[0], 16):
            out_ref[row // 32, row // 16 % 2, p] = value[row : row + 16]


def early_call(owner, tables, record, first, pairs):
    blocks, times, points = record.shape
    count = tables.shape[1] // 32
    out = pl.pallas_call(
        functools.partial(early_kernel, first),
        in_specs=[
            pl.BlockSpec(memory_space=pltpu.SMEM),
            pl.BlockSpec(memory_space=pl.ANY),
            pl.BlockSpec(memory_space=pl.ANY),
        ],
        out_specs=pl.BlockSpec(memory_space=pltpu.VMEM),
        out_shape=jax.ShapeDtypeStruct((count, 2, pairs, 16, points), jnp.bfloat16),
        scratch_shapes=[
            pltpu.VMEM((32 * count, 256), jnp.bfloat16),
            pltpu.VMEM((pairs, 2, times, points), jnp.bfloat16),
            pltpu.SemaphoreType.DMA,
            pltpu.SemaphoreType.DMA((pairs,)),
        ],
        compiler_params=pltpu.CompilerParams(vmem_limit_bytes=58 * MIB),
        cost_estimate=pl.CostEstimate(
            flops=2 * 32 * count * 256 * points * pairs, bytes_accessed=pairs * MIB, transcendentals=0
        ),
        name="early",
    )(owner, tables, record)
    return out.reshape(count, 2, 16 * pairs, points)


def spectra_kernel(owner_ref, table_ref, record_ref, *outs):
    points = record_ref.shape[-1]
    width = 256
    for start in range(0, points, width):
        cols = pl.ds(start, width)
        rows = record_ref[:, :, cols].reshape(256, width)
        value = jnp.dot(table_ref[0], rows, preferred_element_type=jnp.float32)
        value = value.astype(jnp.bfloat16)
        row = 0
        for out in outs:
            for chunk in range(2):
                for c in range(2):
                    out[chunk, c, 0, :, cols] = value[row : row + 16]
                    row += 16


def spectra_call(owner, tables, record):
    blocks, times, points = record.shape
    pairs = blocks // 2
    count = tables.shape[1] // 32
    outs = pl.pallas_call(
        spectra_kernel,
        grid_spec=pltpu.PrefetchScalarGridSpec(
            num_scalar_prefetch=1,
            grid=(pairs,),
            in_specs=[
                pl.BlockSpec((1, 32 * count, 256), lambda p, owner: (owner[0], 0, 0)),
                pl.BlockSpec((2, times, points), lambda p, owner: (p, 0, 0)),
            ],
            out_specs=[
                pl.BlockSpec((2, 2, 1, 16, points), lambda p, owner: (0, 0, p, 0, 0))
            ]
            * (count // 2),
        ),
        out_shape=[jax.ShapeDtypeStruct((2, 2, pairs, 16, points), jnp.bfloat16)] * (count // 2),
        compiler_params=pltpu.CompilerParams(vmem_limit_bytes=16 * MIB),
        cost_estimate=pl.CostEstimate(
            flops=2 * 32 * count * 256 * points * pairs,
            bytes_accessed=(6 + count) * MIB,
            transcendentals=0,
        ),
        name="spectra",
    )(owner, tables, record)
    return [out.reshape(2, 2, 16 * pairs, points) for out in outs]


def nt_dot(a, b):
    return lax.dot_general(a, b, (((1,), (1,)), ((), ())), preferred_element_type=jnp.float32)


def swap_rows(x):
    half = x.shape[0] // 2
    return jnp.concatenate([x[half:], x[:half]], axis=0)


def swap_lanes(x):
    half = x.shape[1] // 2
    return jnp.concatenate([x[:, half:], x[:, :half]], axis=1)


def upper():
    row = lax.broadcasted_iota(jnp.int32, (32, 256), 0)
    return row >= lax.broadcasted_iota(jnp.int32, (32, 256), 1) // 8


def unpack(packed):
    row_f = lax.broadcasted_iota(jnp.int32, (32, 8, 256), 1)
    same = row_f == lax.broadcasted_iota(jnp.int32, (32, 8, 256), 2) % 8
    spread = jnp.where(same, jnp.broadcast_to(packed[:, None, :], (32, 8, 256)), 0.0)
    turned = spread.reshape(256, 256).T.reshape(32, 8, 256).sum(axis=1)
    row = lax.broadcasted_iota(jnp.int32, (32, 256), 0)
    column = lax.broadcasted_iota(jnp.int32, (32, 256), 1) // 8
    real = jnp.where(row >= column, packed, turned)
    imag = jnp.where(row < column, packed, jnp.where(row > column, -turned, 0.0))
    return real, imag


def gram_kernel(parts, owner_ref, weights_ref, *rest):
    out_ref = rest[-1]
    first = owner_ref[0] == 0
    weights = weights_ref[...]
    row_f = lax.broadcasted_iota(jnp.int32, (256, 256), 0) % 8
    col_f = lax.broadcasted_iota(jnp.int32, (256, 256), 1) % 8
    same = row_f == col_f
    for i in range(out_ref.shape[0]):
        x0, x1 = (jnp.concatenate([ref[i, c] for ref in rest[:parts]], axis=0) for c in range(2))
        w0 = (x0.astype(jnp.float32) * weights).astype(jnp.bfloat16)
        w1 = (x1.astype(jnp.float32) * weights).astype(jnp.bfloat16)
        real = nt_dot(x0, w0) + nt_dot(x1, w1)
        imag = nt_dot(x0, w1) - nt_dot(x1, w0)
        both = []
        for value in (real, imag):
            value = jnp.where(same, value, 0.0).reshape(32, 8, 256).sum(axis=1)
            both.append(jnp.where(first, value, swap_rows(swap_lanes(value))))
        out_ref[i] = jnp.where(upper(), both[0], both[1])


def gram_call(owner, weights, rows):
    chunks, _, _, points = rows[0].shape
    return pl.pallas_call(
        functools.partial(gram_kernel, len(rows)),
        in_specs=[pl.BlockSpec(memory_space=pltpu.SMEM)]
        + [pl.BlockSpec(memory_space=pltpu.VMEM)] * (1 + len(rows)),
        out_specs=pl.BlockSpec(memory_space=pltpu.VMEM),
        out_shape=jax.ShapeDtypeStruct((chunks, 32, 256), jnp.float32),
        compiler_params=pltpu.CompilerParams(vmem_limit_bytes=16 * MIB),
        cost_estimate=pl.CostEstimate(
            flops=8 * 256 * 256 * points * chunks,
            bytes_accessed=2 * MIB * chunks,
            transcendentals=0,
        ),
        name="gram",
    )(owner, weights, *rows)


def eliminate(products, scale):
    lane = lax.broadcasted_iota(jnp.int32, (8, 128), 1)
    lane_f = lane % 8
    lane_row = lane // 8
    sub = lax.broadcasted_iota(jnp.int32, (8, 128), 0)
    states = []
    for real, imag in products:
        real, imag = real * scale, imag * scale
        grid = []
        for q in range(4):
            half = slice(128 * (q % 2), 128 * (q % 2) + 128)
            top, bottom = (real, imag) if q < 2 else (-imag, real)
            grid.append(
                [top[8 * s : 8 * s + 8, half] for s in range(4)]
                + [bottom[8 * s : 8 * s + 8, half] for s in range(4)]
            )
        states.append(grid)
    def column_of(grid, k):
        take = lane_f + 8 * (k % 16)
        return [
            jnp.take_along_axis(grid[k // 16][s], take, axis=1, mode="promise_in_bounds")
            for s in range(8)
        ]

    def row_of(blocks, k):
        return jnp.broadcast_to(blocks[k // 8][k % 8 : k % 8 + 1], (8, 128))

    ahead = [{k: column_of(grid, k) for k in range(AHEAD)} for grid in states]
    for k in range(64):
        q0, group = divmod(k, 16)
        s0, r0 = divmod(k, 8)
        for grid, later in zip(states, ahead):
            column = later.pop(k)
            if k + AHEAD < 64:
                later[k + AHEAD] = column_of(grid, k + AHEAD)
            inverse = 1.0 / row_of(column, k)
            factors = {n: row_of(column, n) * inverse for n in later}
            column[s0] = jnp.where(sub == r0, 1.0, column[s0])
            for n, blocks in later.items():
                blocks[s0] = jnp.where(sub == r0, 0.0, blocks[s0])
                later[n] = [blocks[s] - column[s] * factors[n] for s in range(8)]
            for q in range(q0, 4):
                factor = row_of(grid[q], k) * inverse
                keep = sub != r0
                if q == q0:
                    factor = jnp.where(lane_row > group, factor, 0.0)
                    keep = keep | (lane_row <= group)
                grid[q][s0] = jnp.where(keep, grid[q][s0], 0.0)
                for s in range(8):
                    grid[q][s] = grid[q][s] - column[s] * factor
    return states


def diagonal(grid):
    lane_row = lax.broadcasted_iota(jnp.int32, (8, 128), 1) // 8
    sub = lax.broadcasted_iota(jnp.int32, (8, 128), 0)
    out = []
    for q in range(4):
        total = jnp.zeros((8, 128), jnp.float32)
        for s in (2 * q, 2 * q + 1):
            total = total + jnp.where(lane_row + 16 * q == sub + 8 * s, grid[q][s], 0.0)
        out.append(total.sum(axis=0, keepdims=True))
    return out


def lower_rows(grid, pivots):
    lane_row = lax.broadcasted_iota(jnp.int32, (8, 128), 1) // 8
    sub = lax.broadcasted_iota(jnp.int32, (8, 128), 0)
    halves = []
    for q in (2, 3):
        root = lax.rsqrt(pivots[q])
        blocks = []
        for s in range(8):
            row, column = lane_row + 16 * q, sub + 8 * s
            value = jnp.where(column < row, grid[q][s], jnp.where(column == row, 1.0, 0.0))
            blocks.append(value * root)
        halves.append(jnp.concatenate(blocks, axis=0))
    return jnp.concatenate(halves, axis=1)


def build_maps(scale, owner, sums_ref, energies_ref, maps_ref):
    chunks = sums_ref.shape[0]
    states = eliminate([unpack(sums_ref[i]) for i in range(chunks)], scale)
    out_row = lax.broadcasted_iota(jnp.int32, (256, 256), 0)
    lane = lax.broadcasted_iota(jnp.int32, (256, 256), 1)
    same = out_row // 32 == lane % 8
    order = (same & (out_row % 32 == lane // 8)).astype(jnp.bfloat16)
    b_row = lax.broadcasted_iota(jnp.int32, (32, 256), 0)
    b_lane = lax.broadcasted_iota(jnp.int32, (32, 256), 1) // 8
    spread = (b_row == (b_lane + 16 * owner) % 32).astype(jnp.bfloat16)
    for i, grid in enumerate(states):
        pivots = diagonal(grid)
        for q in range(4):
            energies_ref[i, q : q + 1, :] = pivots[q]
        full = lower_rows(grid, pivots)
        high = full.astype(jnp.bfloat16)
        low = (full - high.astype(jnp.float32)).astype(jnp.bfloat16)
        for level, value in enumerate((high, low)):
            rows = nt_dot(order, value).astype(jnp.bfloat16)
            for c in range(2):
                wide = jnp.dot(
                    rows[:, 32 * c : 32 * c + 32], spread, preferred_element_type=jnp.float32
                )
                wide = jnp.where(same, wide, 0.0)
                at = 256 * (2 * c + level)
                maps_ref[i, 0, :, at : at + 256] = (wide if c == 0 else -wide).astype(jnp.bfloat16)
                at = 256 * (2 * (1 - c) + level)
                maps_ref[i, 1, :, at : at + 256] = wide.astype(jnp.bfloat16)


def apply_maps(maps_ref, i, refs, at, modes_ref, first):
    width = 256
    for start in range(0, refs[0].shape[-1], width):
        cols = pl.ds(start, width)
        x0, x1 = (jnp.concatenate([ref[at, c, :, cols] for ref in refs], axis=0) for c in range(2))
        stacked = jnp.concatenate([x0, x0, x1, x1], axis=0)
        for c in range(2):
            value = jnp.dot(maps_ref[i, c], stacked, preferred_element_type=jnp.float32)
            modes_ref[first : first + 8, c, :, cols] = value.astype(jnp.bfloat16).reshape(
                8, 32, width
            )


def factor_kernel(scale, owner_ref, sums_ref, maps_ref, energies_ref):
    build_maps(scale, owner_ref[0], sums_ref, energies_ref, maps_ref)


def factor_call(owner, sums, point_count):
    chunks = sums.shape[0]
    return pl.pallas_call(
        functools.partial(factor_kernel, 1.0 / point_count),
        in_specs=[
            pl.BlockSpec(memory_space=pltpu.SMEM),
            pl.BlockSpec(memory_space=pltpu.VMEM),
        ],
        out_specs=[pl.BlockSpec(memory_space=pltpu.VMEM)] * 2,
        out_shape=[
            jax.ShapeDtypeStruct((chunks, 2, 256, 1024), jnp.bfloat16),
            jax.ShapeDtypeStruct((chunks, 4, 128), jnp.float32),
        ],
        compiler_params=pltpu.CompilerParams(vmem_limit_bytes=16 * MIB),
        cost_estimate=pl.CostEstimate(
            flops=1 << 30, bytes_accessed=2 * MIB * chunks, transcendentals=0
        ),
        name="factor",
    )(owner, sums)


def apply_kernel(count, maps_ref, *rest):
    apply_maps(maps_ref, 0, rest[:count], 0, rest[-1], 0)


def solve_kernel(scale, parts, owner_ref, sums_ref, *rest):
    modes_ref, energies_ref, maps_ref = rest[-3:]

    @pl.when(pl.program_id(0) == 0)
    def factor():
        build_maps(scale, owner_ref[0], sums_ref, energies_ref, maps_ref)

    for i in range(sums_ref.shape[0]):
        apply_maps(maps_ref, i, rest[:parts], i, modes_ref, 8 * i)


def row_specs(rows, tiles, chunks, first):
    return [
        pl.BlockSpec(
            (chunks, *part.shape[1:3], part.shape[3] // tiles), lambda t: (first, 0, 0, t)
        )
        for part in rows
    ]


def modes_shape(total_chunks, points):
    return jax.ShapeDtypeStruct((8 * total_chunks, 2, 32, points), jnp.bfloat16)


def apply_call(maps, index, rows, modes, base, total_chunks, tiles=2):
    points = rows[0].shape[-1]
    operands = [maps, *rows]
    in_specs = [pl.BlockSpec((1, 2, 256, 1024), lambda t: (index, 0, 0, 0))]
    in_specs += row_specs(rows, tiles, 1, index)
    aliases = {}
    if modes is not None:
        aliases = {len(operands): 0}
        in_specs.append(pl.BlockSpec(memory_space=pl.ANY))
        operands.append(modes)
    return pl.pallas_call(
        functools.partial(apply_kernel, len(rows)),
        grid=(tiles,),
        in_specs=in_specs,
        out_specs=pl.BlockSpec((8, 2, 32, points // tiles), lambda t: (base, 0, 0, t)),
        out_shape=modes_shape(total_chunks, points),
        input_output_aliases=aliases,
        compiler_params=pltpu.CompilerParams(vmem_limit_bytes=16 * MIB),
        cost_estimate=pl.CostEstimate(
            flops=16 * 256 * 256 * points, bytes_accessed=4 * MIB, transcendentals=0
        ),
        name="apply",
    )(*operands)


def solve_call(owner, sums, rows, modes, base, total_chunks, point_count, tiles=2):
    chunks, _, _, points = rows[0].shape
    return pl.pallas_call(
        functools.partial(solve_kernel, 1.0 / point_count, len(rows)),
        grid=(tiles,),
        in_specs=[
            pl.BlockSpec(memory_space=pltpu.SMEM),
            pl.BlockSpec((chunks, 32, 256), lambda t: (0, 0, 0)),
            *row_specs(rows, tiles, chunks, 0),
            pl.BlockSpec(memory_space=pl.ANY),
        ],
        out_specs=[
            pl.BlockSpec(
                (8 * chunks, 2, 32, points // tiles), lambda t: (base // chunks, 0, 0, t)
            ),
            pl.BlockSpec((chunks, 4, 128), lambda t: (0, 0, 0)),
        ],
        out_shape=[
            modes_shape(total_chunks, points),
            jax.ShapeDtypeStruct((chunks, 4, 128), jnp.float32),
        ],
        scratch_shapes=[pltpu.VMEM((chunks, 2, 256, 1024), jnp.bfloat16)],
        input_output_aliases={2 + len(rows): 0},
        compiler_params=pltpu.CompilerParams(vmem_limit_bytes=20 * MIB),
        cost_estimate=pl.CostEstimate(
            flops=16 * 256 * 256 * points * chunks,
            bytes_accessed=chunks * 4 * MIB,
            transcendentals=0,
        ),
        name="solve",
    )(owner, sums, *rows, modes)


def after(value, *others):
    return lax.optimization_barrier((value, *others))[0]


def involution(pairs):
    return pairs + [(b, a) for a, b in pairs]


STEPS = (
    ("core", involution([(0, 1)])),
    ("y", involution([(0, 1), (2, 3)])),
    ("y", involution([(0, 3), (1, 2)])),
    ("z", involution([(0, 1), (2, 3), (4, 5), (6, 7)])),
    ("z", involution([(0, 5), (1, 4), (2, 7), (3, 6)])),
    ("z", involution([(1, 2), (3, 4), (5, 6), (7, 0)])),
    ("xh", involution([(0, 1)])),
)
ROUND = (("z", "xh"), involution([(2 * z, 2 * (z ^ 1) + 1) for z in range(8)]))


def add_step(value, step):
    axis, pairs = step
    return value + lax.ppermute(value, axis, pairs)


def local(record, weights):
    points = record.shape[-1]
    space = 1
    for axis in FINE[:-1]:
        space *= lax.axis_size(axis)
    owner = lax.axis_index("blk").astype(jnp.int32).reshape(1)
    wide = weights.reshape(1, points)
    tables = np.stack([pair_table(0), pair_table(1)])
    part = lambda a, b: jnp.asarray(tables[:, a:b])
    swap = lambda s: lax.ppermute(s, "blk", [(0, 1), (1, 0)])
    gram = functools.partial(gram_call, owner, wide)
    solve = functools.partial(solve_call, owner, total_chunks=4, point_count=points * space)

    away_a = early_call(owner, part(128, 192), record, 0, 2)
    peer_a = swap(away_a)
    away_b = early_call(owner, part(128, 192), after(record, away_a), 2, 6)
    peer_b = swap(away_b)
    rest = np.concatenate([tables[:, 192:], tables[:, :128]], axis=1)
    away_cd, own_ab, own_cd = spectra_call(
        owner, jnp.asarray(rest), after(record, peer_a, away_b)
    )
    rows_ab = [own_ab, peer_a, peer_b]
    rows_cd = [own_cd, swap(away_cd)]

    ab = gram(rows_ab)
    for step in STEPS[:6] + (ROUND,):
        ab = add_step(ab, step)
    cd = gram(lax.optimization_barrier((*rows_cd, ab))[:2])
    for step in STEPS[:3]:
        cd = add_step(cd, step)
    maps, pivots_ab = factor_call(owner, after(ab, cd), points * space)
    for step in STEPS[3:5]:
        cd = add_step(cd, step)
    maps = after(maps, cd)
    modes = apply_call(maps, 0, rows_ab, None, 0, 4)
    cd = add_step(after(cd, maps), STEPS[5])
    modes = apply_call(after(maps, cd), 1, rows_ab, modes, 1, 4)
    cd = add_step(cd, STEPS[6])
    modes, pivots_cd = solve(cd, rows_cd, modes, 2)
    pivots = jnp.concatenate([pivots_ab, pivots_cd], axis=0)
    energies = pivots.reshape(-1, 64, 8).transpose(0, 2, 1).reshape(-1, 64)
    return (modes, energies)


def solution(mesh):
    fine = Mesh(mesh.devices.reshape(8, 4, 2, 2, 2), FINE)
    return jax.shard_map(
        local,
        mesh=fine,
        in_specs=(P("blk", None, FINE[:-1]), P(FINE[:-1])),
        out_specs=(P("blk", None, None, FINE[:-1]), P("blk", None)),
        check_vma=False,
    )
```

```python
import functools
import math

import jax
import jax.numpy as jnp
import numpy as np
from jax import lax
from jax.experimental import pallas as pl
from jax.experimental.pallas import tpu as pltpu
from jax.sharding import Mesh
from jax.sharding import PartitionSpec as P

NF = 64
NT = 128
GROUPS = (1, 1, 2)
FINE = ("z", "y", "xh", "core", "blk")
AHEAD = 3
MIB = 1024 * 1024
HEAVY = 40_000_000_000


def spectral_table():
    time_index = np.arange(NT, dtype=np.int32)
    freq_index = np.arange(NF, dtype=np.int32)
    step = np.float32(2.0 * math.pi / NT)
    phases = (freq_index[:, None] * time_index[None, :] % NT).astype(np.float32) * step
    window = np.float32(0.5) - np.float32(0.5) * np.cos(time_index.astype(np.float32) * step)
    norm = np.sqrt(np.sum(window * window))
    rows_cos = window * np.cos(phases) / norm
    rows_sin = -window * np.sin(phases) / norm
    return np.stack([rows_cos, rows_sin], axis=1).astype(jnp.bfloat16)


def pair_table(first_owner):
    table = spectral_table().reshape(2, 4, 8, 2, NT)
    out = np.zeros((2, 4, 2, 2, 8, 2, NT), dtype=table.dtype)
    for b in range(2):
        out[:, :, :, b, :, b, :] = table.transpose(0, 1, 3, 2, 4)
    if first_owner:
        out = out[::-1]
    return np.ascontiguousarray(out).reshape(256, 256)


def early_kernel(first, owner_ref, tables_ref, record_ref, out_ref, table, rows, table_sem, sems):
    pairs, _, _, points = rows.shape
    head = pltpu.make_async_copy(tables_ref.at[owner_ref[0]], table, table_sem)
    head.start()
    copies = [
        pltpu.make_async_copy(
            record_ref.at[pl.ds(2 * (first + p), 2)], rows.at[p], sems.at[p]
        )
        for p in range(pairs)
    ]
    for p in range(min(4, pairs)):
        copies[p].start()
    head.wait()
    left = table[...]
    for p in range(pairs):
        copies[p].wait()
        if p + 4 < pairs:
            copies[p + 4].start()
        value = jnp.dot(
            left, rows[p].reshape(256, points), preferred_element_type=jnp.float32
        ).astype(jnp.bfloat16)
        for row in range(0, value.shape[0], 16):
            out_ref[row // 32, row // 16 % 2, p] = value[row : row + 16]


def early_call(owner, tables, record, first, pairs):
    blocks, times, points = record.shape
    count = tables.shape[1] // 32
    out = pl.pallas_call(
        functools.partial(early_kernel, first),
        in_specs=[
            pl.BlockSpec(memory_space=pltpu.SMEM),
            pl.BlockSpec(memory_space=pl.ANY),
            pl.BlockSpec(memory_space=pl.ANY),
        ],
        out_specs=pl.BlockSpec(memory_space=pltpu.VMEM),
        out_shape=jax.ShapeDtypeStruct((count, 2, pairs, 16, points), jnp.bfloat16),
        scratch_shapes=[
            pltpu.VMEM((32 * count, 256), jnp.bfloat16),
            pltpu.VMEM((pairs, 2, times, points), jnp.bfloat16),
            pltpu.SemaphoreType.DMA,
            pltpu.SemaphoreType.DMA((pairs,)),
        ],
        compiler_params=pltpu.CompilerParams(vmem_limit_bytes=58 * MIB),
        cost_estimate=pl.CostEstimate(
            flops=HEAVY // 2, bytes_accessed=pairs * MIB, transcendentals=0
        ),
        name="early",
    )(owner, tables, record)
    return out.reshape(count, 2, 16 * pairs, points)


def spectra_kernel(owner_ref, table_ref, record_ref, *outs):
    points = record_ref.shape[-1]
    width = 256
    for start in range(0, points, width):
        cols = pl.ds(start, width)
        rows = record_ref[:, :, cols].reshape(256, width)
        value = jnp.dot(table_ref[0], rows, preferred_element_type=jnp.float32)
        value = value.astype(jnp.bfloat16)
        row = 0
        for out in outs:
            for chunk in range(out.shape[0]):
                for c in range(2):
                    out[chunk, c, 0, :, cols] = value[row : row + 16]
                    row += 16


def spectra_call(owner, tables, record, chunks):
    blocks, times, points = record.shape
    pairs = blocks // 2
    count = tables.shape[1] // 32
    outs = pl.pallas_call(
        spectra_kernel,
        grid_spec=pltpu.PrefetchScalarGridSpec(
            num_scalar_prefetch=1,
            grid=(pairs,),
            in_specs=[
                pl.BlockSpec((1, 32 * count, 256), lambda p, owner: (owner[0], 0, 0)),
                pl.BlockSpec((2, times, points), lambda p, owner: (p, 0, 0)),
            ],
            out_specs=[
                pl.BlockSpec((n, 2, 1, 16, points), lambda p, owner: (0, 0, p, 0, 0))
                for n in chunks
            ],
        ),
        out_shape=[
            jax.ShapeDtypeStruct((n, 2, pairs, 16, points), jnp.bfloat16) for n in chunks
        ],
        compiler_params=pltpu.CompilerParams(vmem_limit_bytes=16 * MIB),
        cost_estimate=pl.CostEstimate(
            flops=HEAVY, bytes_accessed=(6 + count) * MIB, transcendentals=0
        ),
        name="spectra",
    )(owner, tables, record)
    return [out.reshape(n, 2, 16 * pairs, points) for n, out in zip(chunks, outs)]


def nt_dot(a, b):
    return lax.dot_general(a, b, (((1,), (1,)), ((), ())), preferred_element_type=jnp.float32)


def swap_rows(x):
    half = x.shape[0] // 2
    return jnp.concatenate([x[half:], x[:half]], axis=0)


def swap_lanes(x):
    half = x.shape[1] // 2
    return jnp.concatenate([x[:, half:], x[:, :half]], axis=1)


def upper():
    row = lax.broadcasted_iota(jnp.int32, (32, 256), 0)
    return row >= lax.broadcasted_iota(jnp.int32, (32, 256), 1) // 8


def unpack(packed):
    row_f = lax.broadcasted_iota(jnp.int32, (32, 8, 256), 1)
    same = row_f == lax.broadcasted_iota(jnp.int32, (32, 8, 256), 2) % 8
    spread = jnp.where(same, jnp.broadcast_to(packed[:, None, :], (32, 8, 256)), 0.0)
    turned = spread.reshape(256, 256).T.reshape(32, 8, 256).sum(axis=1)
    row = lax.broadcasted_iota(jnp.int32, (32, 256), 0)
    column = lax.broadcasted_iota(jnp.int32, (32, 256), 1) // 8
    real = jnp.where(row >= column, packed, turned)
    imag = jnp.where(row < column, packed, jnp.where(row > column, -turned, 0.0))
    return real, imag


def chunk_rows(refs, parts, c):
    return jnp.concatenate([refs[ref][chunk, c] for ref, chunk in parts], axis=0)


def gram_kernel(plan, prior, owner_ref, core_ref, weights_ref, *refs):
    first = owner_ref[0] == 0
    weights = weights_ref[...]
    row_f = lax.broadcasted_iota(jnp.int32, (256, 256), 0) % 8
    col_f = lax.broadcasted_iota(jnp.int32, (256, 256), 1) % 8
    same = row_f == col_f
    packed = [refs[-3][0]] if prior else []
    for parts in plan:
        x0, x1 = (chunk_rows(refs, parts, c) for c in range(2))
        w0 = (x0.astype(jnp.float32) * weights).astype(jnp.bfloat16)
        w1 = (x1.astype(jnp.float32) * weights).astype(jnp.bfloat16)
        real = nt_dot(x0, w0) + nt_dot(x1, w1)
        imag = nt_dot(x0, w1) - nt_dot(x1, w0)
        both = []
        for value in (real, imag):
            value = jnp.where(same, value, 0.0).reshape(32, 8, 256).sum(axis=1)
            both.append(jnp.where(first, value, swap_rows(swap_lanes(value))))
        packed.append(jnp.where(upper(), both[0], both[1]))
    if len(packed) == 1:
        refs[-1][0] = packed[0]
    else:
        core = core_ref[0] == 0
        refs[-2][0] = jnp.where(core, packed[0], packed[1])
        refs[-1][0] = jnp.where(core, packed[1], packed[0])


def plan_of(rows):
    arrays = []
    for parts in rows:
        for array, _ in parts:
            if not any(array is other for other in arrays):
                arrays.append(array)
    index = lambda array: next(i for i, other in enumerate(arrays) if other is array)
    return arrays, [[(index(array), chunk) for array, chunk in parts] for parts in rows]


def gram_call(place, weights, rows, prior=None, flops=1 << 30):
    arrays, plan = plan_of(rows)
    points = arrays[0].shape[-1]
    results = len(rows) + (prior is not None)
    operands = [*place, weights, *arrays]
    if prior is not None:
        operands.append(prior)
    return pl.pallas_call(
        functools.partial(gram_kernel, plan, prior is not None),
        in_specs=[pl.BlockSpec(memory_space=pltpu.SMEM)] * 2
        + [pl.BlockSpec(memory_space=pltpu.VMEM)] * (len(operands) - 2),
        out_specs=[pl.BlockSpec(memory_space=pltpu.VMEM)] * results,
        out_shape=[jax.ShapeDtypeStruct((1, 32, 256), jnp.float32)] * results,
        compiler_params=pltpu.CompilerParams(vmem_limit_bytes=16 * MIB),
        cost_estimate=pl.CostEstimate(
            flops=flops,
            bytes_accessed=2 * MIB * len(rows),
            transcendentals=0,
        ),
        name="gram",
    )(*operands)


def eliminate(products, scale):
    lane = lax.broadcasted_iota(jnp.int32, (8, 128), 1)
    lane_f = lane % 8
    lane_row = lane // 8
    sub = lax.broadcasted_iota(jnp.int32, (8, 128), 0)
    states = []
    for real, imag in products:
        real, imag = real * scale, imag * scale
        grid = []
        for q in range(4):
            half = slice(128 * (q % 2), 128 * (q % 2) + 128)
            top, bottom = (real, imag) if q < 2 else (-imag, real)
            grid.append(
                [top[8 * s : 8 * s + 8, half] for s in range(4)]
                + [bottom[8 * s : 8 * s + 8, half] for s in range(4)]
            )
        states.append(grid)
    def column_of(grid, k):
        take = lane_f + 8 * (k % 16)
        return [
            jnp.take_along_axis(grid[k // 16][s], take, axis=1, mode="promise_in_bounds")
            for s in range(8)
        ]

    def row_of(blocks, k):
        return jnp.broadcast_to(blocks[k // 8][k % 8 : k % 8 + 1], (8, 128))

    ahead = [{k: column_of(grid, k) for k in range(AHEAD)} for grid in states]
    for k in range(64):
        q0, group = divmod(k, 16)
        s0, r0 = divmod(k, 8)
        for grid, later in zip(states, ahead):
            column = later.pop(k)
            if k + AHEAD < 64:
                later[k + AHEAD] = column_of(grid, k + AHEAD)
            inverse = 1.0 / row_of(column, k)
            factors = {n: row_of(column, n) * inverse for n in later}
            column[s0] = jnp.where(sub == r0, 1.0, column[s0])
            for n, blocks in later.items():
                blocks[s0] = jnp.where(sub == r0, 0.0, blocks[s0])
                later[n] = [blocks[s] - column[s] * factors[n] for s in range(8)]
            for q in range(q0, 4):
                factor = row_of(grid[q], k) * inverse
                keep = sub != r0
                if q == q0:
                    factor = jnp.where(lane_row > group, factor, 0.0)
                    keep = keep | (lane_row <= group)
                grid[q][s0] = jnp.where(keep, grid[q][s0], 0.0)
                for s in range(8):
                    grid[q][s] = grid[q][s] - column[s] * factor
    return states


def diagonal(grid):
    lane_row = lax.broadcasted_iota(jnp.int32, (8, 128), 1) // 8
    sub = lax.broadcasted_iota(jnp.int32, (8, 128), 0)
    out = []
    for q in range(4):
        total = jnp.zeros((8, 128), jnp.float32)
        for s in (2 * q, 2 * q + 1):
            total = total + jnp.where(lane_row + 16 * q == sub + 8 * s, grid[q][s], 0.0)
        out.append(total.sum(axis=0, keepdims=True))
    return out


def lower_rows(grid, pivots):
    lane_row = lax.broadcasted_iota(jnp.int32, (8, 128), 1) // 8
    sub = lax.broadcasted_iota(jnp.int32, (8, 128), 0)
    halves = []
    for q in (2, 3):
        root = lax.rsqrt(pivots[q])
        blocks = []
        for s in range(8):
            row, column = lane_row + 16 * q, sub + 8 * s
            value = jnp.where(column < row, grid[q][s], jnp.where(column == row, 1.0, 0.0))
            blocks.append(value * root)
        halves.append(jnp.concatenate(blocks, axis=0))
    return jnp.concatenate(halves, axis=1)


def by_frequency(pivots):
    sub = lax.broadcasted_iota(jnp.int32, (8, 128), 0)
    lane = lax.broadcasted_iota(jnp.int32, (8, 128), 1)
    out = jnp.zeros((8, 128), jnp.float32)
    for q, vector in enumerate(pivots):
        wide = jnp.broadcast_to(vector, (8, 128))
        turned = jnp.take_along_axis(
            wide, lane % 16 * 8 + sub, axis=1, mode="promise_in_bounds"
        )
        out = jnp.where(lane // 16 == q, turned, out)
    return out[:, :64]


def factor_kernel(scale, sums_ref, out_ref):
    grid = eliminate([unpack(sums_ref[0])], scale)[0]
    pivots = diagonal(grid)
    out_ref[:64, :] = lower_rows(grid, pivots)
    out_ref[64:, :] = jnp.zeros((8, 256), jnp.float32)
    out_ref[64:, :64] = by_frequency(pivots)


def factor_call(sums, point_count):
    return pl.pallas_call(
        functools.partial(factor_kernel, 1.0 / point_count),
        in_specs=[pl.BlockSpec(memory_space=pltpu.VMEM)],
        out_specs=pl.BlockSpec(memory_space=pltpu.VMEM),
        out_shape=jax.ShapeDtypeStruct((72, 256), jnp.float32),
        compiler_params=pltpu.CompilerParams(vmem_limit_bytes=16 * MIB),
        cost_estimate=pl.CostEstimate(flops=1 << 30, bytes_accessed=4 * MIB, transcendentals=0),
        name="factor",
    )(sums)


def build_maps(owner, full, maps_ref):
    out_row = lax.broadcasted_iota(jnp.int32, (256, 256), 0)
    lane = lax.broadcasted_iota(jnp.int32, (256, 256), 1)
    same = out_row // 32 == lane % 8
    order = (same & (out_row % 32 == lane // 8)).astype(jnp.bfloat16)
    b_row = lax.broadcasted_iota(jnp.int32, (32, 256), 0)
    b_lane = lax.broadcasted_iota(jnp.int32, (32, 256), 1) // 8
    spread = (b_row == (b_lane + 16 * owner) % 32).astype(jnp.bfloat16)
    high = full.astype(jnp.bfloat16)
    low = (full - high.astype(jnp.float32)).astype(jnp.bfloat16)
    for level, value in enumerate((high, low)):
        rows = nt_dot(order, value).astype(jnp.bfloat16)
        for c in range(2):
            wide = jnp.dot(
                rows[:, 32 * c : 32 * c + 32], spread, preferred_element_type=jnp.float32
            )
            wide = jnp.where(same, wide, 0.0)
            at = 256 * (2 * c + level)
            maps_ref[0, :, at : at + 256] = (wide if c == 0 else -wide).astype(jnp.bfloat16)
            at = 256 * (2 * (1 - c) + level)
            maps_ref[1, :, at : at + 256] = wide.astype(jnp.bfloat16)


def apply_kernel(base, theirs, plan, energies, owner_ref, core_ref, full_ref, *refs):
    count = max(ref for parts in plan for ref, _ in parts) + 1
    rows, refs = refs[:count], refs[count:]
    if energies:
        others, (modes_ref, energies_ref, small_ref, small_sem) = refs[:3], refs[-7:-3]
    else:
        modes_ref = refs[-4]
    maps_ref, held_ref, sems = refs[-3:]
    core = core_ref[0]
    chosen = 1 - core if theirs else core
    copies = []
    if energies:
        for half, pair in enumerate(((others[0], others[1]), (others[2], full_ref))):
            values = [ref[64:, :64] for ref in pair]
            at = 16 * half
            small_ref[at : at + 8, :] = jnp.where(core == 0, values[0], values[1])
            small_ref[at + 8 : at + 16, :] = jnp.where(core == 0, values[1], values[0])
        copies.append(pltpu.make_async_copy(small_ref, energies_ref, small_sem))
        copies[0].start()
    build_maps(owner_ref[0], full_ref[:64, :], maps_ref)
    points = held_ref.shape[-1]
    width = 256
    piece = points // sems.shape[0]
    target = modes_ref.at[pl.ds(8 * (base + chosen), 8)]
    for part in range(sems.shape[0]):
        for start in range(part * piece, (part + 1) * piece, width):
            cols = pl.ds(start, width)
            x0, x1 = (
                jnp.concatenate(
                    [
                        rows[ref][chosen, c, :, cols]
                        if rows[ref].shape[0] == 2
                        else jnp.where(
                            chosen == 0, rows[ref][0, c, :, cols], rows[other][0, c, :, cols]
                        )
                        for (ref, _), (other, _) in zip(*plan)
                    ],
                    axis=0,
                )
                for c in range(2)
            )
            stacked = jnp.concatenate([x0, x0, x1, x1], axis=0)
            for c in range(2):
                value = jnp.dot(maps_ref[c], stacked, preferred_element_type=jnp.float32)
                held_ref[:, c, :, cols] = value.astype(jnp.bfloat16).reshape(8, 32, width)
        cols = pl.ds(part * piece, piece)
        copy = pltpu.make_async_copy(
            held_ref.at[:, :, :, cols], target.at[:, :, :, cols], sems.at[part]
        )
        copy.start()
        copies.append(copy)
    for copy in copies:
        copy.wait()


def modes_shape(total_chunks, points):
    return jax.ShapeDtypeStruct((8 * total_chunks, 2, 32, points), jnp.bfloat16)


def apply_call(place, full, rows, modes, base, theirs, total_chunks, others=()):
    arrays, plan = plan_of(rows)
    points = arrays[0].shape[-1]
    operands = [*place, full, *arrays, *others]
    in_specs = [pl.BlockSpec(memory_space=pltpu.SMEM)] * 2
    in_specs += [pl.BlockSpec(memory_space=pltpu.VMEM)] * (len(operands) - 2)
    aliases, small = {}, []
    if modes is not None:
        aliases = {len(operands): 0}
        in_specs.append(pl.BlockSpec(memory_space=pl.ANY))
        operands.append(modes)
    out_specs = [pl.BlockSpec(memory_space=pl.ANY)]
    out_shape = [modes_shape(total_chunks, points)]
    if others:
        out_specs.append(pl.BlockSpec(memory_space=pl.ANY))
        out_shape.append(jax.ShapeDtypeStruct((8 * total_chunks, 64), jnp.float32))
        small = [pltpu.VMEM((8 * total_chunks, 64), jnp.float32), pltpu.SemaphoreType.DMA]
    return pl.pallas_call(
        functools.partial(apply_kernel, base, theirs, plan, bool(others)),
        in_specs=in_specs,
        out_specs=out_specs,
        out_shape=out_shape,
        scratch_shapes=small
        + [
            pltpu.VMEM((2, 256, 1024), jnp.bfloat16),
            pltpu.VMEM((8, 2, 32, points), jnp.bfloat16),
            pltpu.SemaphoreType.DMA((6,)),
        ],
        input_output_aliases=aliases,
        compiler_params=pltpu.CompilerParams(vmem_limit_bytes=16 * MIB),
        cost_estimate=pl.CostEstimate(
            flops=16 * 256 * 256 * points, bytes_accessed=4 * MIB, transcendentals=0
        ),
        name="apply",
    )(*operands)


def after(value, *others):
    return lax.optimization_barrier((value, *others))[0]


def involution(pairs):
    return pairs + [(b, a) for a, b in pairs]


CORE = ("core", involution([(0, 1)]))
STEPS = (
    ("y", involution([(0, 1), (2, 3)])),
    ("y", involution([(0, 3), (1, 2)])),
    ("z", involution([(0, 1), (2, 3), (4, 5), (6, 7)])),
    ("z", involution([(0, 2), (1, 3), (4, 6), (5, 7)])),
    ("z", involution([(0, 7), (1, 6), (2, 5), (3, 4)])),
    ("xh", involution([(0, 1)])),
)


def add_step(value, step):
    axis, pairs = step
    return value + lax.ppermute(value, axis, pairs)


def local(record, weights):
    points = record.shape[-1]
    space = 1
    for axis in FINE[:-1]:
        space *= lax.axis_size(axis)
    owner, core = (
        lax.axis_index(axis).astype(jnp.int32).reshape(1) for axis in ("blk", "core")
    )
    place = (owner, core)
    wide = weights.reshape(1, points)
    tables = np.stack([pair_table(0), pair_table(1)])
    part = lambda a, b: jnp.asarray(tables[:, a:b])
    swap = lambda s: lax.ppermute(s, "blk", [(0, 1), (1, 0)])
    cross = lambda value: lax.ppermute(value, *CORE)
    gram = functools.partial(gram_call, place, wide)

    away_a = early_call(owner, part(128, 192), record, 0, 2)
    peer_a = swap(away_a)
    away_b = early_call(owner, part(128, 192), after(record, away_a), 2, 6)
    peer_b = swap(away_b)
    rest = np.concatenate([tables[:, 192:], tables[:, :128]], axis=1)
    away_c, away_d, own_ab, own_cd = spectra_call(
        owner, jnp.asarray(rest), after(record, peer_a, away_b), (1, 1, 2, 2)
    )
    peer_c, peer_d = swap(away_c), swap(away_d)
    rows_ab = [[(own_ab, i), (peer_a, i), (peer_b, i)] for i in range(2)]

    apply = functools.partial(apply_call, place, total_chunks=4)

    ab, other = gram(rows_ab, flops=HEAVY)
    ab = ab + cross(other)
    for step in STEPS[:4]:
        ab = add_step(ab, step)
    peer_c = after(peer_c, ab)
    c = gram([[(own_cd, 0), (peer_c, 0)]])[0]
    ab = add_step(ab, STEPS[4])
    peer_d = after(peer_d, ab)
    cd, other = gram([[(own_cd, 1), (peer_d, 0)]], c)
    rows_cd = [[(own_cd, 0), (peer_c, 0)], [(own_cd, 1), (peer_d, 0)]]
    ab = add_step(ab, STEPS[5])
    cd = cd + cross(other)
    cd = add_step(cd, STEPS[0])
    mine_ab = factor_call(after(ab, cd), points * space)
    theirs_ab = cross(mine_ab)
    for step in STEPS[1:3]:
        cd = add_step(cd, step)
    modes = apply(after(mine_ab, cd), rows_ab, None, 0, False)[0]
    cd = add_step(after(cd, mine_ab), STEPS[3])
    modes = apply(after(theirs_ab, cd), rows_ab, modes, 0, True)[0]
    for step in STEPS[4:]:
        cd = add_step(cd, step)
    mine_cd = factor_call(cd, points * space)
    theirs_cd = cross(mine_cd)
    modes = apply(mine_cd, rows_cd, modes, 2, False)[0]
    return tuple(
        apply(theirs_cd, rows_cd, modes, 2, True, others=(mine_ab, theirs_ab, mine_cd))
    )


def solution(mesh):
    fine = Mesh(mesh.devices.reshape(8, 4, 2, 2, 2), FINE)
    return jax.shard_map(
        local,
        mesh=fine,
        in_specs=(P("blk", None, FINE[:-1]), P(FINE[:-1])),
        out_specs=(P("blk", None, None, FINE[:-1]), P("blk", None)),
        check_vma=False,
    )
```

```python
import functools
import math

import jax
import jax.numpy as jnp
import numpy as np
from jax import lax
from jax.experimental import pallas as pl
from jax.experimental.pallas import tpu as pltpu
from jax.sharding import Mesh
from jax.sharding import PartitionSpec as P

NF = 64
NT = 128
GROUPS = (1, 1, 2)
FINE = ("z", "y", "xh", "core", "blk")
AHEAD = 3
MIB = 1024 * 1024
HEAVY = 40_000_000_000


def spectral_table():
    time_index = np.arange(NT, dtype=np.int32)
    freq_index = np.arange(NF, dtype=np.int32)
    step = np.float32(2.0 * math.pi / NT)
    phases = (freq_index[:, None] * time_index[None, :] % NT).astype(np.float32) * step
    window = np.float32(0.5) - np.float32(0.5) * np.cos(time_index.astype(np.float32) * step)
    norm = np.sqrt(np.sum(window * window))
    rows_cos = window * np.cos(phases) / norm
    rows_sin = -window * np.sin(phases) / norm
    return np.stack([rows_cos, rows_sin], axis=1).astype(jnp.bfloat16)


def pair_table(first_owner):
    table = spectral_table().reshape(2, 4, 8, 2, NT)
    out = np.zeros((2, 4, 2, 2, 8, 2, NT), dtype=table.dtype)
    for b in range(2):
        out[:, :, :, b, :, b, :] = table.transpose(0, 1, 3, 2, 4)
    if first_owner:
        out = out[::-1]
    return np.ascontiguousarray(out).reshape(256, 256)


def early_kernel(first, owner_ref, tables_ref, record_ref, out_ref, table, rows, table_sem, sems):
    pairs, _, _, points = rows.shape
    head = pltpu.make_async_copy(tables_ref.at[owner_ref[0]], table, table_sem)
    head.start()
    copies = [
        pltpu.make_async_copy(
            record_ref.at[pl.ds(2 * (first + p), 2)], rows.at[p], sems.at[p]
        )
        for p in range(pairs)
    ]
    for p in range(min(4, pairs)):
        copies[p].start()
    head.wait()
    left = table[...]
    for p in range(pairs):
        copies[p].wait()
        if p + 4 < pairs:
            copies[p + 4].start()
        value = jnp.dot(
            left, rows[p].reshape(256, points), preferred_element_type=jnp.float32
        ).astype(jnp.bfloat16)
        for row in range(0, value.shape[0], 16):
            out_ref[row // 32, row // 16 % 2, p] = value[row : row + 16]


def early_call(owner, tables, record, first, pairs):
    blocks, times, points = record.shape
    count = tables.shape[1] // 32
    out = pl.pallas_call(
        functools.partial(early_kernel, first),
        in_specs=[
            pl.BlockSpec(memory_space=pltpu.SMEM),
            pl.BlockSpec(memory_space=pl.ANY),
            pl.BlockSpec(memory_space=pl.ANY),
        ],
        out_specs=pl.BlockSpec(memory_space=pltpu.VMEM),
        out_shape=jax.ShapeDtypeStruct((count, 2, pairs, 16, points), jnp.bfloat16),
        scratch_shapes=[
            pltpu.VMEM((32 * count, 256), jnp.bfloat16),
            pltpu.VMEM((pairs, 2, times, points), jnp.bfloat16),
            pltpu.SemaphoreType.DMA,
            pltpu.SemaphoreType.DMA((pairs,)),
        ],
        compiler_params=pltpu.CompilerParams(vmem_limit_bytes=58 * MIB),
        cost_estimate=pl.CostEstimate(
            flops=HEAVY // 2, bytes_accessed=pairs * MIB, transcendentals=0
        ),
        name="early",
    )(owner, tables, record)
    return out.reshape(count, 2, 16 * pairs, points)


def spectra_kernel(owner_ref, table_ref, record_ref, *outs):
    points = record_ref.shape[-1]
    width = 256
    for start in range(0, points, width):
        cols = pl.ds(start, width)
        rows = record_ref[:, :, cols].reshape(256, width)
        value = jnp.dot(table_ref[0], rows, preferred_element_type=jnp.float32)
        value = value.astype(jnp.bfloat16)
        row = 0
        for out in outs:
            for chunk in range(out.shape[0]):
                for c in range(2):
                    out[chunk, c, 0, :, cols] = value[row : row + 16]
                    row += 16


def spectra_call(owner, tables, record, chunks):
    blocks, times, points = record.shape
    pairs = blocks // 2
    count = tables.shape[1] // 32
    outs = pl.pallas_call(
        spectra_kernel,
        grid_spec=pltpu.PrefetchScalarGridSpec(
            num_scalar_prefetch=1,
            grid=(pairs,),
            in_specs=[
                pl.BlockSpec((1, 32 * count, 256), lambda p, owner: (owner[0], 0, 0)),
                pl.BlockSpec((2, times, points), lambda p, owner: (p, 0, 0)),
            ],
            out_specs=[
                pl.BlockSpec((n, 2, 1, 16, points), lambda p, owner: (0, 0, p, 0, 0))
                for n in chunks
            ],
        ),
        out_shape=[
            jax.ShapeDtypeStruct((n, 2, pairs, 16, points), jnp.bfloat16) for n in chunks
        ],
        compiler_params=pltpu.CompilerParams(vmem_limit_bytes=16 * MIB),
        cost_estimate=pl.CostEstimate(
            flops=HEAVY, bytes_accessed=(6 + count) * MIB, transcendentals=0
        ),
        name="spectra",
    )(owner, tables, record)
    return [out.reshape(n, 2, 16 * pairs, points) for n, out in zip(chunks, outs)]


def nt_dot(a, b):
    return lax.dot_general(a, b, (((1,), (1,)), ((), ())), preferred_element_type=jnp.float32)


def swap_rows(x):
    half = x.shape[0] // 2
    return jnp.concatenate([x[half:], x[:half]], axis=0)


def swap_lanes(x):
    half = x.shape[1] // 2
    return jnp.concatenate([x[:, half:], x[:, :half]], axis=1)


def upper():
    row = lax.broadcasted_iota(jnp.int32, (32, 256), 0)
    return row >= lax.broadcasted_iota(jnp.int32, (32, 256), 1) // 8


def unpack(packed):
    row_f = lax.broadcasted_iota(jnp.int32, (32, 8, 256), 1)
    same = row_f == lax.broadcasted_iota(jnp.int32, (32, 8, 256), 2) % 8
    spread = jnp.where(same, jnp.broadcast_to(packed[:, None, :], (32, 8, 256)), 0.0)
    turned = spread.reshape(256, 256).T.reshape(32, 8, 256).sum(axis=1)
    row = lax.broadcasted_iota(jnp.int32, (32, 256), 0)
    column = lax.broadcasted_iota(jnp.int32, (32, 256), 1) // 8
    real = jnp.where(row >= column, packed, turned)
    imag = jnp.where(row < column, packed, jnp.where(row > column, -turned, 0.0))
    return real, imag


def chunk_rows(refs, parts, c):
    return jnp.concatenate([refs[ref][chunk, c] for ref, chunk in parts], axis=0)


def gram_kernel(plan, prior, owner_ref, core_ref, weights_ref, *refs):
    first = owner_ref[0] == 0
    weights = weights_ref[...]
    row_f = lax.broadcasted_iota(jnp.int32, (256, 256), 0) % 8
    col_f = lax.broadcasted_iota(jnp.int32, (256, 256), 1) % 8
    same = row_f == col_f
    packed = [refs[-3][0]] if prior else []
    for parts in plan:
        x0, x1 = (chunk_rows(refs, parts, c) for c in range(2))
        w0 = (x0.astype(jnp.float32) * weights).astype(jnp.bfloat16)
        w1 = (x1.astype(jnp.float32) * weights).astype(jnp.bfloat16)
        real = nt_dot(x0, w0) + nt_dot(x1, w1)
        imag = nt_dot(x0, w1) - nt_dot(x1, w0)
        both = []
        for value in (real, imag):
            value = jnp.where(same, value, 0.0).reshape(32, 8, 256).sum(axis=1)
            both.append(jnp.where(first, value, swap_rows(swap_lanes(value))))
        packed.append(jnp.where(upper(), both[0], both[1]))
    if len(packed) == 1:
        refs[-1][0] = packed[0]
    else:
        core = core_ref[0] == 0
        refs[-2][0] = jnp.where(core, packed[0], packed[1])
        refs[-1][0] = jnp.where(core, packed[1], packed[0])


def plan_of(rows):
    arrays = []
    for parts in rows:
        for array, _ in parts:
            if not any(array is other for other in arrays):
                arrays.append(array)
    index = lambda array: next(i for i, other in enumerate(arrays) if other is array)
    return arrays, [[(index(array), chunk) for array, chunk in parts] for parts in rows]


def gram_call(place, weights, rows, prior=None, flops=1 << 30):
    arrays, plan = plan_of(rows)
    points = arrays[0].shape[-1]
    results = len(rows) + (prior is not None)
    operands = [*place, weights, *arrays]
    if prior is not None:
        operands.append(prior)
    return pl.pallas_call(
        functools.partial(gram_kernel, plan, prior is not None),
        in_specs=[pl.BlockSpec(memory_space=pltpu.SMEM)] * 2
        + [pl.BlockSpec(memory_space=pltpu.VMEM)] * (len(operands) - 2),
        out_specs=[pl.BlockSpec(memory_space=pltpu.VMEM)] * results,
        out_shape=[jax.ShapeDtypeStruct((1, 32, 256), jnp.float32)] * results,
        compiler_params=pltpu.CompilerParams(vmem_limit_bytes=16 * MIB),
        cost_estimate=pl.CostEstimate(
            flops=flops,
            bytes_accessed=2 * MIB * len(rows),
            transcendentals=0,
        ),
        name="gram",
    )(*operands)


def eliminate(products, scale):
    lane = lax.broadcasted_iota(jnp.int32, (8, 128), 1)
    lane_f = lane % 8
    lane_row = lane // 8
    sub = lax.broadcasted_iota(jnp.int32, (8, 128), 0)
    states = []
    for real, imag in products:
        real, imag = real * scale, imag * scale
        grid = []
        for q in range(4):
            half = slice(128 * (q % 2), 128 * (q % 2) + 128)
            top, bottom = (real, imag) if q < 2 else (-imag, real)
            grid.append(
                [top[8 * s : 8 * s + 8, half] for s in range(4)]
                + [bottom[8 * s : 8 * s + 8, half] for s in range(4)]
            )
        states.append(grid)
    def column_of(grid, k):
        take = lane_f + 8 * (k % 16)
        return [
            jnp.take_along_axis(grid[k // 16][s], take, axis=1, mode="promise_in_bounds")
            for s in range(8)
        ]

    def row_of(blocks, k):
        return jnp.broadcast_to(blocks[k // 8][k % 8 : k % 8 + 1], (8, 128))

    ahead = [{k: column_of(grid, k) for k in range(AHEAD)} for grid in states]
    for k in range(64):
        q0, group = divmod(k, 16)
        s0, r0 = divmod(k, 8)
        for grid, later in zip(states, ahead):
            column = later.pop(k)
            if k + AHEAD < 64:
                later[k + AHEAD] = column_of(grid, k + AHEAD)
            inverse = 1.0 / row_of(column, k)
            factors = {n: row_of(column, n) * inverse for n in later}
            column[s0] = jnp.where(sub == r0, 1.0, column[s0])
            for n, blocks in later.items():
                blocks[s0] = jnp.where(sub == r0, 0.0, blocks[s0])
                later[n] = [blocks[s] - column[s] * factors[n] for s in range(8)]
            for q in range(q0, 4):
                factor = row_of(grid[q], k) * inverse
                keep = sub != r0
                if q == q0:
                    factor = jnp.where(lane_row > group, factor, 0.0)
                    keep = keep | (lane_row <= group)
                grid[q][s0] = jnp.where(keep, grid[q][s0], 0.0)
                for s in range(8):
                    grid[q][s] = grid[q][s] - column[s] * factor
    return states


def diagonal(grid):
    lane_row = lax.broadcasted_iota(jnp.int32, (8, 128), 1) // 8
    sub = lax.broadcasted_iota(jnp.int32, (8, 128), 0)
    out = []
    for q in range(4):
        total = jnp.zeros((8, 128), jnp.float32)
        for s in (2 * q, 2 * q + 1):
            total = total + jnp.where(lane_row + 16 * q == sub + 8 * s, grid[q][s], 0.0)
        out.append(total.sum(axis=0, keepdims=True))
    return out


def lower_rows(grid, pivots):
    lane_row = lax.broadcasted_iota(jnp.int32, (8, 128), 1) // 8
    sub = lax.broadcasted_iota(jnp.int32, (8, 128), 0)
    halves = []
    for q in (2, 3):
        root = lax.rsqrt(pivots[q])
        blocks = []
        for s in range(8):
            row, column = lane_row + 16 * q, sub + 8 * s
            value = jnp.where(column < row, grid[q][s], jnp.where(column == row, 1.0, 0.0))
            blocks.append(value * root)
        halves.append(jnp.concatenate(blocks, axis=0))
    return jnp.concatenate(halves, axis=1)


def by_frequency(pivots):
    sub = lax.broadcasted_iota(jnp.int32, (8, 128), 0)
    lane = lax.broadcasted_iota(jnp.int32, (8, 128), 1)
    out = jnp.zeros((8, 128), jnp.float32)
    for q, vector in enumerate(pivots):
        wide = jnp.broadcast_to(vector, (8, 128))
        turned = jnp.take_along_axis(
            wide, lane % 16 * 8 + sub, axis=1, mode="promise_in_bounds"
        )
        out = jnp.where(lane // 16 == q, turned, out)
    return out[:, :64]


def factor_kernel(scale, sums_ref, out_ref):
    grid = eliminate([unpack(sums_ref[0])], scale)[0]
    pivots = diagonal(grid)
    out_ref[:64, :] = lower_rows(grid, pivots)
    out_ref[64:, :] = jnp.zeros((8, 256), jnp.float32)
    out_ref[64:, :64] = by_frequency(pivots)


def factor_call(sums, point_count):
    return pl.pallas_call(
        functools.partial(factor_kernel, 1.0 / point_count),
        in_specs=[pl.BlockSpec(memory_space=pltpu.VMEM)],
        out_specs=pl.BlockSpec(memory_space=pltpu.VMEM),
        out_shape=jax.ShapeDtypeStruct((72, 256), jnp.float32),
        compiler_params=pltpu.CompilerParams(vmem_limit_bytes=16 * MIB),
        cost_estimate=pl.CostEstimate(flops=1 << 30, bytes_accessed=4 * MIB, transcendentals=0),
        name="factor",
    )(sums)


def build_maps(owner, full, maps_ref):
    out_row = lax.broadcasted_iota(jnp.int32, (256, 256), 0)
    lane = lax.broadcasted_iota(jnp.int32, (256, 256), 1)
    same = out_row // 32 == lane % 8
    order = (same & (out_row % 32 == lane // 8)).astype(jnp.bfloat16)
    high = full.astype(jnp.bfloat16)
    low = (full - high.astype(jnp.float32)).astype(jnp.bfloat16)
    both = jnp.concatenate([high, low], axis=0)
    rows = nt_dot(order, both).astype(jnp.bfloat16)
    from_row = lax.broadcasted_iota(jnp.int32, (128, 1024), 0)
    to_lane = lax.broadcasted_iota(jnp.int32, (128, 1024), 1)
    b_lane = (to_lane % 256 // 8 + 16 * owner) % 32
    level, c = to_lane // 256 % 2, to_lane // 512
    spread = (from_row == 64 * level + 32 * c + b_lane).astype(jnp.bfloat16)
    wide = jnp.dot(rows, spread, preferred_element_type=jnp.float32)
    for at in range(0, 1024, 256):
        part = jnp.where(same, wide[:, at : at + 256], 0.0)
        maps_ref[0, :, at : at + 256] = (part if at < 512 else -part).astype(jnp.bfloat16)
        swapped = (at + 512) % 1024
        maps_ref[1, :, swapped : swapped + 256] = part.astype(jnp.bfloat16)


def apply_kernel(base, theirs, plan, column, energies, owner_ref, core_ref, full_ref, *refs):
    count = max(ref for parts in plan for ref, _ in parts) + 1
    rows, refs = refs[:count], refs[count:]
    if energies:
        others, (modes_ref, energies_ref, small_ref, small_sem) = refs[:3], refs[-7:-3]
    else:
        modes_ref = refs[-4]
    maps_ref, held_ref, sems = refs[-3:]
    core = core_ref[0]
    chosen = 1 - core if theirs else core
    copies = []
    if energies:
        for half, pair in enumerate(((others[0], others[1]), (others[2], full_ref))):
            values = [ref[64:, :64] for ref in pair]
            at = 16 * half
            small_ref[at : at + 8, :] = jnp.where(core == 0, values[0], values[1])
            small_ref[at + 8 : at + 16, :] = jnp.where(core == 0, values[1], values[0])
        copies.append(pltpu.make_async_copy(small_ref, energies_ref, small_sem))
        copies[0].start()
    build_maps(owner_ref[0], full_ref[:64, :], maps_ref)
    points = held_ref.shape[-1]
    width = 256
    piece = points // sems.shape[0]
    target = modes_ref.at[pl.ds(8 * (base + chosen), 8)]
    for part in range(sems.shape[0]):
        for start in range(part * piece, (part + 1) * piece, width):
            cols = pl.ds(start, width)
            read = pl.ds(column + start, width)
            x0, x1 = (
                jnp.concatenate(
                    [
                        rows[ref][chosen, c, :, read]
                        if rows[ref].shape[0] == 2
                        else jnp.where(
                            chosen == 0, rows[ref][0, c, :, read], rows[other][0, c, :, read]
                        )
                        for (ref, _), (other, _) in zip(*plan)
                    ],
                    axis=0,
                )
                for c in range(2)
            )
            stacked = jnp.concatenate([x0, x0, x1, x1], axis=0)
            for c in range(2):
                value = jnp.dot(maps_ref[c], stacked, preferred_element_type=jnp.float32)
                held_ref[:, c, :, cols] = value.astype(jnp.bfloat16).reshape(8, 32, width)
        cols = pl.ds(part * piece, piece)
        copy = pltpu.make_async_copy(
            held_ref.at[:, :, :, cols],
            target.at[:, :, :, pl.ds(column + part * piece, piece)],
            sems.at[part],
        )
        copy.start()
        copies.append(copy)
    for copy in copies:
        copy.wait()


def modes_shape(total_chunks, points):
    return jax.ShapeDtypeStruct((8 * total_chunks, 2, 32, points), jnp.bfloat16)


def apply_call(
    place, full, rows, modes, base, theirs, total_chunks, others=(), column=0, width=None
):
    arrays, plan = plan_of(rows)
    points = arrays[0].shape[-1]
    width = width or points
    operands = [*place, full, *arrays, *others]
    in_specs = [pl.BlockSpec(memory_space=pltpu.SMEM)] * 2
    in_specs += [pl.BlockSpec(memory_space=pltpu.VMEM)] * (len(operands) - 2)
    aliases, small = {}, []
    if modes is not None:
        aliases = {len(operands): 0}
        in_specs.append(pl.BlockSpec(memory_space=pl.ANY))
        operands.append(modes)
    out_specs = [pl.BlockSpec(memory_space=pl.ANY)]
    out_shape = [modes_shape(total_chunks, points)]
    if others:
        out_specs.append(pl.BlockSpec(memory_space=pl.ANY))
        out_shape.append(jax.ShapeDtypeStruct((8 * total_chunks, 64), jnp.float32))
        small = [pltpu.VMEM((8 * total_chunks, 64), jnp.float32), pltpu.SemaphoreType.DMA]
    return pl.pallas_call(
        functools.partial(apply_kernel, base, theirs, plan, column, bool(others)),
        in_specs=in_specs,
        out_specs=out_specs,
        out_shape=out_shape,
        scratch_shapes=small
        + [
            pltpu.VMEM((2, 256, 1024), jnp.bfloat16),
            pltpu.VMEM((8, 2, 32, width), jnp.bfloat16),
            pltpu.SemaphoreType.DMA((width // 256,)),
        ],
        input_output_aliases=aliases,
        compiler_params=pltpu.CompilerParams(vmem_limit_bytes=16 * MIB),
        cost_estimate=pl.CostEstimate(
            flops=16 * 256 * 256 * width, bytes_accessed=2 * MIB, transcendentals=0
        ),
        name="apply",
    )(*operands)


def after(value, *others):
    return lax.optimization_barrier((value, *others))[0]


def involution(pairs):
    return pairs + [(b, a) for a, b in pairs]


CORE = ("core", involution([(0, 1)]))
STEPS = (
    ("y", involution([(0, 1), (2, 3)])),
    ("y", involution([(0, 3), (1, 2)])),
    ("z", involution([(0, 1), (2, 3), (4, 5), (6, 7)])),
    ("z", involution([(0, 2), (1, 3), (4, 6), (5, 7)])),
    ("z", involution([(0, 7), (1, 6), (2, 5), (3, 4)])),
    ("xh", involution([(0, 1)])),
)


def add_step(value, step):
    axis, pairs = step
    return value + lax.ppermute(value, axis, pairs)


def local(record, weights):
    points = record.shape[-1]
    space = 1
    for axis in FINE[:-1]:
        space *= lax.axis_size(axis)
    owner, core = (
        lax.axis_index(axis).astype(jnp.int32).reshape(1) for axis in ("blk", "core")
    )
    place = (owner, core)
    wide = weights.reshape(1, points)
    tables = np.stack([pair_table(0), pair_table(1)])
    part = lambda a, b: jnp.asarray(tables[:, a:b])
    swap = lambda s: lax.ppermute(s, "blk", [(0, 1), (1, 0)])
    cross = lambda value: lax.ppermute(value, *CORE)
    gram = functools.partial(gram_call, place, wide)

    away_a = early_call(owner, part(128, 192), record, 0, 2)
    peer_a = swap(away_a)
    away_b = early_call(owner, part(128, 192), after(record, away_a), 2, 6)
    peer_b = swap(away_b)
    rest = np.concatenate([tables[:, 192:], tables[:, :128]], axis=1)
    away_c, away_d, own_ab, own_cd = spectra_call(
        owner, jnp.asarray(rest), after(record, peer_a, away_b), (1, 1, 2, 2)
    )
    peer_c, peer_d = swap(away_c), swap(away_d)
    rows_ab = [[(own_ab, i), (peer_a, i), (peer_b, i)] for i in range(2)]

    apply = functools.partial(apply_call, place, total_chunks=4)

    ab, other = gram(rows_ab, flops=HEAVY)
    ab = ab + cross(other)
    for step in STEPS[:4]:
        ab = add_step(ab, step)
    peer_c = after(peer_c, ab)
    c = gram([[(own_cd, 0), (peer_c, 0)]])[0]
    ab = add_step(ab, STEPS[4])
    peer_d = after(peer_d, ab)
    cd, other = gram([[(own_cd, 1), (peer_d, 0)]], c)
    rows_cd = [[(own_cd, 0), (peer_c, 0)], [(own_cd, 1), (peer_d, 0)]]
    cd = cd + cross(other)
    ab = add_step(after(ab, cd), STEPS[5])
    cd = add_step(cd, STEPS[0])
    mine_ab = factor_call(after(ab, cd), points * space)
    theirs_ab = cross(mine_ab)
    half, modes = points // 2, None
    for step, theirs, column in (
        (1, False, 0),
        (2, False, half),
        (3, True, 0),
        (4, True, half),
    ):
        cd = add_step(cd, STEPS[step])
        full = after(theirs_ab if theirs else mine_ab, cd)
        modes = apply(full, rows_ab, modes, 0, theirs, column=column, width=half)[0]
    cd = add_step(cd, STEPS[5])
    mine_cd = factor_call(cd, points * space)
    theirs_cd = cross(mine_cd)
    modes = apply(mine_cd, rows_cd, modes, 2, False)[0]
    return tuple(
        apply(theirs_cd, rows_cd, modes, 2, True, others=(mine_ab, theirs_ab, mine_cd))
    )


def solution(mesh):
    fine = Mesh(mesh.devices.reshape(8, 4, 2, 2, 2), FINE)
    return jax.shard_map(
        local,
        mesh=fine,
        in_specs=(P("blk", None, FINE[:-1]), P(FINE[:-1])),
        out_specs=(P("blk", None, None, FINE[:-1]), P("blk", None)),
        check_vma=False,
    )
```
